32 devices in a mesh: fsdp: 8 (over y, x, core), tensor: 4 (over z).
Axes of the slice: x: 2, y: 2, z: 4, core: 2. Of those that a mesh axis runs over, the one named last changes fastest.
Arguments:
- out_grad: bfloat16 [256, 8192], P(('fsdp', 'tensor')), may hold values from -6 to 6
- live_rows: int32 [32], P(('fsdp', 'tensor')), may hold values from 1 to 8, as said below
- gate_pre: bfloat16 [256, 12288], P('fsdp', 'tensor'), may hold values from -8 to 8
- up_pre: bfloat16 [256, 12288], P('fsdp', 'tensor'), may hold values from -6 to 6
- down_weight: bfloat16 [12288, 8192], P('tensor', 'fsdp'), may hold values from -0.15625 to 0.15625
- tile_mask: int32 [96, 64], P('tensor'), may hold values from 0 to 1, as said below
Outputs:
- d_gate: bfloat16 [256, 12288], P('fsdp', 'tensor')
- d_up: bfloat16 [256, 12288], P('fsdp', 'tensor')
- d_weight: bfloat16 [12288, 8192], P('tensor', 'fsdp')
The draws below stay inside these ranges and needn't reach their ends.
Inputs may be any that keep to these rules, and one draw needn't show every extreme that they name: `tile_mask`: each device's shard of 24 x 8 tiles holds 1 to 4 kept tiles; in every draw the shards of some tensor index all hold exactly 4, and every tensor index has a shard holding 4. `live_rows`: some device has all 8 rows live in every draw.
All inputs are finite; a program needn't handle non-finite values.
Results may differ from the reference program's by a relative error of at most 0.015.
Values may be sent and summed in bfloat16 or wider, within the bound.
A program may use at most 64 MiB of HBM per device.

```python
import math
import jax
import jax.numpy as jnp
from jax import lax

D = 8192
FF = 12288
BLK = 128
CAP = 4
TOK_DEV = 8
ROWS = 32
TOKENS = 256
FB = 96
DB = 64
ROWB = 24
COLB = 8
N_FSDP = 8


def draw_tile_mask(key, part):
    tensor_count = FB // ROWB
    fsdp_count = DB // COLB
    local_count = ROWB * COLB
    key_one, key_two, key_three, key_four = jax.random.split(jax.random.fold_in(key, 11), 4)
    counts = jax.random.randint(key_one, (tensor_count, fsdp_count), 1, CAP + 1)
    full_row = jax.random.randint(key_two, (), 0, tensor_count)
    full_col = jax.random.randint(key_three, (tensor_count,), 0, fsdp_count)
    tensor_ids = jnp.arange(tensor_count)[:, None]
    fsdp_ids = jnp.arange(fsdp_count)[None, :]
    counts = jnp.where((tensor_ids == full_row) | (fsdp_ids == full_col[:, None]), CAP, counts)
    scores = jax.random.randint(key_four, (tensor_count, fsdp_count, local_count), 0, 1 << 20) * local_count + jnp.arange(local_count)
    order = jnp.argsort(scores, axis=-1)
    ranks = jnp.argsort(order, axis=-1)
    chosen = (ranks < counts[:, :, None]).astype(jnp.int32)
    chosen = chosen.reshape(tensor_count, fsdp_count, ROWB, COLB).transpose(0, 2, 1, 3)
    return chosen.reshape(tensor_count * ROWB, fsdp_count * COLB)


def draw_live_rows(key, part):
    device_count = TOKENS // TOK_DEV
    key_one, key_two = jax.random.split(jax.random.fold_in(key, 23))
    counts = jax.random.randint(key_one, (device_count,), 1, TOK_DEV + 1)
    full_device = jax.random.randint(key_two, (), 0, device_count)
    return jnp.where(jnp.arange(device_count) == full_device, TOK_DEV, counts).astype(jnp.int32)


def spiked(drawn, own_key, source, target, blocks, factor):
    owner, partner = [(jnp.arange(drawn.shape[axis_at]) // (drawn.shape[axis_at] // blocks)).reshape([-1 if axis == axis_at else 1 for axis in range(drawn.ndim)]) for axis_at in (source, target)]
    chosen = jax.random.permutation(own_key, blocks)[partner]
    strong = (owner == chosen) | (owner == (partner + blocks // 2) % blocks)
    return jnp.where(strong, factor * drawn, drawn)


def shard_levels(own_key, extent, pieces, least, largest):
    level = 1.0
    for axis_at, shards_of in pieces:
        heights = jax.random.uniform(jax.random.fold_in(jax.random.fold_in(own_key, 6), axis_at), (shards_of,), jnp.float32, least / len(pieces), largest / len(pieces))
        level = level * jnp.repeat(jnp.exp(heights), extent[axis_at] // shards_of).reshape((-1,) + (1,) * (len(extent) - 1 - axis_at))
    return level


def scatter_about(stream_key, extent, spread, bound, pieces=(), held_as=jnp.bfloat16):
    drawn = jax.random.normal(stream_key, extent, jnp.float32) * spread
    if len(pieces) > 0:
        drawn = shard_levels(stream_key, extent, pieces, -0.22, 0.18) * drawn
    return jnp.clip(drawn, min=-bound, max=bound).astype(held_as)


def bell_draw_with(stream_key, extent, spread, limit, pieces, heavy, kind=jnp.bfloat16):
    values = spread * jax.random.normal(stream_key, extent, jnp.float32)
    if pieces:
        values = values * shard_levels(stream_key, extent, pieces, -0.22, 0.18)
    return jnp.clip(spiked(values, jax.random.fold_in(stream_key, 3), *heavy), -limit, limit).astype(kind)


def setup_inputs(seed: int = 0) -> dict:
    key_list = jax.random.split(jax.random.key(seed), 7)
    return {
        "out_grad": bell_draw_with(key_list[0], (TOKENS, D), 1.0, 6.0, ((0, 32),), (0, 1, 32, 2.75)),
        "live_rows": draw_live_rows(jax.random.fold_in(key_list[6], 71), 0),
        "gate_pre": scatter_about(key_list[2], (TOKENS, FF), 1.5, 8.0, ((0, 8), (1, 4))),
        "up_pre": scatter_about(key_list[3], (TOKENS, FF), 1.0, 6.0, ((0, 8), (1, 4))),
        "down_weight": scatter_about(key_list[4], (FF, D), (D // 5) ** -0.5, 0.15625, ((0, 4), (1, 8))),
        "tile_mask": draw_tile_mask(jax.random.fold_in(key_list[6], 71), 0),
    }


def reference(out_grad, live_rows, gate_pre, up_pre, down_weight, tile_mask):
    live_mask = jnp.arange(TOK_DEV, dtype=jnp.int32)[None, :] < live_rows[:, None]
    masked_grad = jnp.where(live_mask.reshape(TOKENS, 1), out_grad, jnp.zeros_like(out_grad))
    tile_gate = tile_mask.astype(jnp.bfloat16)[:, None, :, None]
    masked_weight = (down_weight.reshape(FB, BLK, DB, BLK) * tile_gate).reshape(FF, D)
    d_hidden = jnp.dot(masked_grad, masked_weight.T, preferred_element_type=jnp.float32)
    gate_value = gate_pre.astype(jnp.float32)
    up_value = up_pre.astype(jnp.float32)
    sigmoid_gate = jax.nn.sigmoid(gate_value)
    hidden = (gate_value * sigmoid_gate * up_value).astype(jnp.bfloat16)
    d_up = (d_hidden * gate_value * sigmoid_gate).astype(jnp.bfloat16)
    d_gate = (d_hidden * up_value * sigmoid_gate * (1.0 + gate_value * (1.0 - sigmoid_gate))).astype(jnp.bfloat16)
    grad_scale = 1.0 / math.sqrt(TOKENS)
    mask_float = tile_mask.astype(jnp.float32)[:, None, :, None]

    def add_group(running, group_pair):
        hidden_group, grad_group = group_pair
        partial_sum = jnp.dot(hidden_group.T, grad_group, preferred_element_type=jnp.float32) * grad_scale
        partial_sum = (partial_sum.reshape(FB, BLK, DB, BLK) * mask_float).reshape(FF, D)
        rounded = lax.optimization_barrier(partial_sum.astype(jnp.bfloat16))
        return (running + rounded.astype(jnp.float32), None)
    running, _ = lax.scan(add_group, jnp.zeros((FF, D), jnp.float32), (hidden.reshape(N_FSDP, ROWS, FF), masked_grad.reshape(N_FSDP, ROWS, D)))
    return (d_gate, d_up, running.astype(jnp.bfloat16))
```

```python
import functools
import math

import jax
import jax.numpy as jnp
from jax import lax
from jax.experimental import pallas as pl
from jax.experimental.pallas import tpu as pltpu
from jax.sharding import PartitionSpec as P

BLK = 128
CAP = 4
MESH = pl.DeviceIdType.MESH
F32 = jnp.float32
BF16 = jnp.bfloat16


def tile_lists(mask, row_blocks, cols):
    shift = cols.bit_length() - 1
    row_count, lanes = mask.shape
    empty = row_count * cols
    row_id = lax.broadcasted_iota(jnp.int32, mask.shape, 0)
    lane = lax.broadcasted_iota(jnp.int32, mask.shape, 1)
    code = jnp.where(mask == 1, row_id * cols + (lane & (cols - 1)), empty)
    shard = lax.shift_right_logical(lane, shift)
    out_row = lax.broadcasted_iota(jnp.int32, (16, BLK), 0)
    out_lane = lax.broadcasted_iota(jnp.int32, (16, BLK), 1)
    found = jnp.full((16, BLK), empty, jnp.int32)
    slot = out_row & (CAP - 1)
    for g in range(lanes // cols):
        own = jnp.where(shard == g, code, empty)
        for k in range(CAP):
            least = jnp.min(jnp.min(own, axis=0, keepdims=True), axis=1, keepdims=True)
            found = jnp.where((slot == k) & (out_lane == g), least, found)
            own = jnp.where(own == least, empty, own)
    row = jnp.minimum(lax.shift_right_logical(found, shift), row_blocks - 1)
    live = jnp.where(found < empty, 1, 0)
    return jnp.where(out_row < CAP, row, jnp.where(out_row < 2 * CAP, found & (cols - 1), live))


def exchange_kernel(
    fs, ts, cols, scale,
    live_ref, grad_ref, gate_ref, up_ref, mask_ref, w_hbm,
    pr_out, dw_out, idx_out,
    chunk, chunk_in, panel, z_send, z_in, hid, hid_send, hid_in, prod, prod_in, w_vmem, idx_v, idx_s,
    w_sem, idx_sem, i_send, i_recv, a_send, a_recv, b_send, b_recv, h_send, h_recv, p_send, p_recv,
):
    f = lax.axis_index("fsdp")
    t = lax.axis_index("tensor")
    tok = grad_ref.shape[0]
    row_blocks, rows = hid.shape[0], hid.shape[1]
    compact = cols > CAP
    held = z_in.shape[1]

    def f_peer(j):
        return lax.rem(f + j, fs)

    def t_peer(j):
        return lax.rem(t + j, ts)

    def tile_row(k, g):
        return idx_s[t, k, g]

    def tile_col(u, k):
        return idx_s[u, CAP + k, f]

    barrier = pltpu.get_barrier_semaphore()
    for j in range(1, fs):
        pl.semaphore_signal(barrier, inc=1, device_id={"fsdp": f_peer(j)}, device_id_type=MESH)
    for j in range(1, ts):
        pl.semaphore_signal(barrier, inc=1, device_id={"tensor": t_peer(j)}, device_id_type=MESH)
    w_copies = []
    for c in range(cols):
        copy = pltpu.make_async_copy(w_hbm.at[:, :, c * BLK : (c + 1) * BLK], w_vmem.at[c], w_sem.at[c])
        copy.start()
        w_copies.append(copy)

    live = lax.broadcasted_iota(jnp.int32, (tok, BLK), 0) < live_ref[0]
    for g in range(fs):
        parts = []
        for c in range(cols):
            at = (g * cols + c) * BLK
            parts.append(jnp.where(live, grad_ref[:, at : at + BLK].astype(F32), 0.0))
        chunk[g] = jnp.concatenate(parts, axis=0).astype(BF16)
    lists = tile_lists(mask_ref[...], row_blocks, cols)
    idx_out[...] = lists
    idx_v[t] = lists

    pl.semaphore_wait(barrier, fs - 1 + ts - 1)

    def over_fsdp(src, dst, send, recv):
        copies = []
        for j in range(1, fs):
            copy = pltpu.make_async_remote_copy(
                src_ref=src.at[f_peer(j)],
                dst_ref=dst.at[f],
                send_sem=send.at[j],
                recv_sem=recv.at[j],
                device_id={"fsdp": f_peer(j)},
                device_id_type=MESH,
            )
            copy.start()
            copies.append(copy)
        return copies

    a_copies = over_fsdp(chunk, chunk_in, a_send, a_recv)
    i_copies = []
    for j in range(1, ts):
        copy = pltpu.make_async_remote_copy(
            src_ref=idx_v.at[t],
            dst_ref=idx_v.at[t],
            send_sem=i_send.at[j],
            recv_sem=i_recv.at[j],
            device_id={"tensor": t_peer(j)},
            device_id_type=MESH,
        )
        copy.start()
        i_copies.append(copy)
    chunk_in[f] = chunk[f]

    for r in range(row_blocks):
        gate = gate_ref[:, r * BLK : (r + 1) * BLK].astype(F32)
        up = up_ref[:, r * BLK : (r + 1) * BLK].astype(F32)
        hid[r] = (gate * jax.nn.sigmoid(gate) * up).astype(BF16)

    for copy in i_copies:
        copy.wait_recv()
    idx_copy = pltpu.make_async_copy(idx_v, idx_s, idx_sem)
    idx_copy.start()

    for copy in a_copies:
        copy.wait_recv()
    wide = [chunk_in[g].astype(F32) for g in range(fs)]
    for c in range(cols):
        panel[c] = jnp.concatenate([w[c * tok : (c + 1) * tok] for w in wide], axis=0).astype(BF16)
    idx_copy.wait()

    b_copies = []
    for j in range(1, ts):
        if compact:
            for k in range(CAP):
                z_send[j, k] = panel[tile_col(t_peer(j), k)]
        copy = pltpu.make_async_remote_copy(
            src_ref=z_send.at[j] if compact else panel,
            dst_ref=z_in.at[t],
            send_sem=b_send.at[j],
            recv_sem=b_recv.at[j],
            device_id={"tensor": t_peer(j)},
            device_id_type=MESH,
        )
        copy.start()
        b_copies.append(copy)
    for k in range(held):
        z_in[t, k] = panel[tile_col(t, k)] if compact else panel[k]

    for g in range(fs):
        for k in range(CAP):
            hid_send[g, k] = hid[tile_row(k, g)]
    h_copies = over_fsdp(hid_send, hid_in, h_send, h_recv)
    hid_in[f] = hid_send[f]

    for copy in w_copies:
        copy.wait()
    for copy in b_copies:
        copy.wait_recv()
    grads = []
    for k in range(CAP):
        col = tile_col(t, k)
        slot = k if compact else col
        wide = [z_in[u, slot].astype(F32) for u in range(ts)]
        pieces = [w[g * tok : (g + 1) * tok] for g in range(fs) for w in wide]
        grad = jnp.concatenate(pieces, axis=0).astype(BF16)
        grads.append(grad)
        tile = w_vmem[col, tile_row(k, f)]
        out = lax.dot_general(grad, tile, (((1,), (1,)), ((), ())), preferred_element_type=F32)
        out = out.astype(BF16)
        for g in range(fs):
            prod[g, k] = out[g * rows : (g + 1) * rows]
    p_copies = over_fsdp(prod, prod_in, p_send, p_recv)
    prod_in[f] = prod[f]

    for copy in h_copies:
        copy.wait_recv()
    for k in range(CAP):
        left = jnp.concatenate([hid_in[g, k] for g in range(fs)], axis=0)
        total = lax.dot_general(left, grads[k], (((0,), (0,)), ((), ())), preferred_element_type=F32)
        dw_out[k] = (total * scale).astype(BF16)
    for copy in p_copies:
        copy.wait_recv()
    pr_out[...] = prod_in[...]
    for copy in i_copies + a_copies + b_copies + h_copies + p_copies:
        copy.wait_send()


def finish_kernel(
    fs, idx_ref, prod_ref, dw_ref, gate_ref, up_ref, d_gate, d_up, d_weight, acc, blank, z_sem, t_sem
):
    row_blocks = acc.shape[0]
    blank[...] = jnp.zeros_like(blank)
    fills = []
    for r in range(row_blocks):
        fill = pltpu.make_async_copy(blank, d_weight.at[pl.ds(r * BLK, BLK)], z_sem.at[r])
        fill.start()
        fills.append(fill)
    acc[...] = jnp.zeros_like(acc)
    for g in range(fs):
        for k in range(CAP):
            row = idx_ref[k, g]
            weight = idx_ref[2 * CAP + k, g].astype(F32)
            acc[row] += prod_ref[g, k].astype(F32) * weight
    for r in range(row_blocks):
        at = slice(r * BLK, (r + 1) * BLK)
        gate = gate_ref[:, at].astype(F32)
        up = up_ref[:, at].astype(F32)
        sig = jax.nn.sigmoid(gate)
        d_hidden = acc[r]
        d_up[:, at] = (d_hidden * gate * sig).astype(BF16)
        d_gate[:, at] = (d_hidden * up * sig * (1.0 + gate * (1.0 - sig))).astype(BF16)
    for fill in fills:
        fill.wait()
    f = lax.axis_index("fsdp")

    def place(k):
        row_at = pl.multiple_of(idx_ref[k, f] * BLK, BLK)
        col_at = pl.multiple_of(idx_ref[CAP + k, f] * BLK, BLK)
        return pltpu.make_async_copy(
            dw_ref.at[k], d_weight.at[pl.ds(row_at, BLK), pl.ds(col_at, BLK)], t_sem.at[k]
        )

    for k in range(CAP):
        @pl.when(idx_ref[2 * CAP + k, f] > 0)
        def _():
            place(k).start()

    for k in range(CAP):
        @pl.when(idx_ref[2 * CAP + k, f] > 0)
        def _():
            place(k).wait()


def per_device(out_grad, live_rows, gate_pre, up_pre, down_weight, tile_mask):
    fs = lax.axis_size("fsdp")
    ts = lax.axis_size("tensor")
    tok = out_grad.shape[0]
    rows = gate_pre.shape[0]
    row_blocks = tile_mask.shape[0]
    cols = down_weight.shape[1] // BLK
    held = min(cols, CAP)
    scale = 1.0 / math.sqrt(rows * fs)
    mask = tile_mask
    if row_blocks % 8:
        mask = jnp.pad(tile_mask, ((0, 8 - row_blocks % 8), (0, 0)))
    vmem = pl.BlockSpec(memory_space=pltpu.VMEM)
    smem = pl.BlockSpec(memory_space=pltpu.SMEM)
    hbm = pl.BlockSpec(memory_space=pltpu.HBM)
    slots = (fs, CAP, rows, BLK)
    dma = pltpu.SemaphoreType.DMA
    prod, tiles, lists = pl.pallas_call(
        functools.partial(exchange_kernel, fs, ts, cols, scale),
        out_shape=(
            jax.ShapeDtypeStruct(slots, BF16),
            jax.ShapeDtypeStruct((CAP, BLK, BLK), BF16),
            jax.ShapeDtypeStruct((16, BLK), jnp.int32),
        ),
        in_specs=[smem, vmem, vmem, vmem, vmem, hbm],
        out_specs=(vmem, vmem, vmem),
        scratch_shapes=[
            pltpu.VMEM((fs, cols * tok, BLK), BF16),
            pltpu.VMEM((fs, cols * tok, BLK), BF16),
            pltpu.VMEM((cols, fs * tok, BLK), BF16),
            pltpu.VMEM((ts, held, fs * tok, BLK), BF16),
            pltpu.VMEM((ts, held, fs * tok, BLK), BF16),
            pltpu.VMEM((row_blocks, rows, BLK), BF16),
            pltpu.VMEM(slots, BF16),
            pltpu.VMEM(slots, BF16),
            pltpu.VMEM(slots, BF16),
            pltpu.VMEM(slots, BF16),
            pltpu.VMEM((cols, row_blocks, BLK, BLK), BF16),
            pltpu.VMEM((ts, 16, BLK), jnp.int32),
            pltpu.SMEM((ts, 16, BLK), jnp.int32),
            dma((cols,)),
            dma,
            dma((ts,)),
            dma((ts,)),
            dma((fs,)),
            dma((fs,)),
            dma((ts,)),
            dma((ts,)),
            dma((fs,)),
            dma((fs,)),
            dma((fs,)),
            dma((fs,)),
        ],
        compiler_params=pltpu.CompilerParams(
            collective_id=0, has_side_effects=True, vmem_limit_bytes=48 * 1024 * 1024
        ),
        name="exchange",
    )(live_rows, out_grad, gate_pre, up_pre, mask, down_weight.reshape(row_blocks, BLK, cols * BLK))
    return pl.pallas_call(
        functools.partial(finish_kernel, fs),
        out_shape=(
            jax.ShapeDtypeStruct(gate_pre.shape, BF16),
            jax.ShapeDtypeStruct(up_pre.shape, BF16),
            jax.ShapeDtypeStruct(down_weight.shape, BF16),
        ),
        in_specs=[smem, vmem, vmem, vmem, vmem],
        out_specs=(vmem, vmem, hbm),
        scratch_shapes=[
            pltpu.VMEM((row_blocks, rows, BLK), F32),
            pltpu.VMEM((BLK, down_weight.shape[1]), BF16),
            dma((row_blocks,)),
            dma((CAP,)),
        ],
        compiler_params=pltpu.CompilerParams(vmem_limit_bytes=32 * 1024 * 1024),
        name="finish",
    )(lists, prod, tiles, gate_pre, up_pre)


def solution(mesh):
    return jax.shard_map(
        per_device,
        mesh=mesh,
        in_specs=(
            P(("fsdp", "tensor"), None),
            P(("fsdp", "tensor")),
            P("fsdp", "tensor"),
            P("fsdp", "tensor"),
            P("tensor", "fsdp"),
            P("tensor", None),
        ),
        out_specs=(P("fsdp", "tensor"), P("fsdp", "tensor"), P("tensor", "fsdp")),
        check_vma=False,
    )
```

```python
import functools
import math

import jax
import jax.numpy as jnp
from jax import lax
from jax.experimental import pallas as pl
from jax.experimental.pallas import tpu as pltpu
from jax.sharding import PartitionSpec as P

BLK = 128
CAP = 4
MESH = pl.DeviceIdType.MESH
F32 = jnp.float32
BF16 = jnp.bfloat16


def tile_lists(mask, row_blocks, cols):
    shift = cols.bit_length() - 1
    row_count, lanes = mask.shape
    empty = row_count * cols
    row_id = lax.broadcasted_iota(jnp.int32, mask.shape, 0)
    lane = lax.broadcasted_iota(jnp.int32, mask.shape, 1)
    code = jnp.where(mask == 1, row_id * cols + (lane & (cols - 1)), empty)
    shard = lax.shift_right_logical(lane, shift)
    out_row = lax.broadcasted_iota(jnp.int32, (16, BLK), 0)
    out_lane = lax.broadcasted_iota(jnp.int32, (16, BLK), 1)
    found = jnp.full((16, BLK), empty, jnp.int32)
    slot = out_row & (CAP - 1)
    for g in range(lanes // cols):
        own = jnp.where(shard == g, code, empty)
        for k in range(CAP):
            least = jnp.min(jnp.min(own, axis=0, keepdims=True), axis=1, keepdims=True)
            found = jnp.where((slot == k) & (out_lane == g), least, found)
            own = jnp.where(own == least, empty, own)
    row = jnp.minimum(lax.shift_right_logical(found, shift), row_blocks - 1)
    live = jnp.where(found < empty, 1, 0)
    return jnp.where(out_row < CAP, row, jnp.where(out_row < 2 * CAP, found & (cols - 1), live))


def exchange_kernel(
    fs, ts, cols, scale,
    live_ref, grad_hbm, gate_hbm, up_hbm, mask_hbm, w_hbm,
    pr_out, dw_out, idx_out,
    grad_ref, gate_ref, up_ref, mask_ref, dw,
    chunk, chunk_in, panel, z_send, z_in, hid, hid_send, hid_in, prod, prod_in, w_vmem, idx_v, idx_s,
    in_sem, out_sem, w_sem, idx_sem, i_send, i_recv, a_send, a_recv, b_send, b_recv, h_send, h_recv, p_send, p_recv,
):
    f = lax.axis_index("fsdp")
    t = lax.axis_index("tensor")
    tok = grad_ref.shape[0]
    row_blocks, rows = hid.shape[0], hid.shape[1]
    compact = cols > CAP
    groups, per_z = z_in.shape[0], z_in.shape[2]
    per_p = prod.shape[2]

    def f_peer(j):
        return lax.rem(f + j, fs)

    def t_peer(j):
        return lax.rem(t + j, ts)

    def tile_row(k, g):
        return idx_s[t, k, g]

    def tile_col(u, k):
        return idx_s[u, CAP + k, f]

    loads = [
        pltpu.make_async_copy(src, dst, in_sem.at[n])
        for n, (src, dst) in enumerate(
            ((grad_hbm, grad_ref), (mask_hbm, mask_ref), (gate_hbm, gate_ref), (up_hbm, up_ref))
        )
    ]
    for copy in loads:
        copy.start()
    barrier = pltpu.get_barrier_semaphore()
    for j in range(1, fs):
        pl.semaphore_signal(barrier, inc=1, device_id={"fsdp": f_peer(j)}, device_id_type=MESH)
    for j in range(1, ts):
        pl.semaphore_signal(barrier, inc=1, device_id={"tensor": t_peer(j)}, device_id_type=MESH)

    live = lax.broadcasted_iota(jnp.int32, (tok, BLK), 0) < live_ref[0]
    loads[0].wait()
    for g in range(fs):
        parts = []
        for c in range(cols):
            at = (g * cols + c) * BLK
            parts.append(jnp.where(live, grad_ref[:, at : at + BLK].astype(F32), 0.0))
        chunk[g] = jnp.concatenate(parts, axis=0).astype(BF16)

    pl.semaphore_wait(barrier, fs - 1 + ts - 1)

    def remote(src, dst, send, recv, peer):
        copy = pltpu.make_async_remote_copy(
            src_ref=src, dst_ref=dst, send_sem=send, recv_sem=recv, device_id=peer, device_id_type=MESH
        )
        copy.start()
        return copy

    def over_fsdp(src, dst, send, recv):
        return [
            remote(src.at[f_peer(j)], dst.at[f], send.at[j], recv.at[j], {"fsdp": f_peer(j)})
            for j in range(1, fs)
        ]

    a_copies = over_fsdp(chunk, chunk_in, a_send, a_recv)
    loads[1].wait()
    lists = tile_lists(mask_ref[...], row_blocks, cols)
    idx_v[t] = lists
    outs = [pltpu.make_async_copy(idx_v.at[t], idx_out, out_sem.at[0])]
    outs[0].start()
    i_copies = [
        remote(idx_v.at[t], idx_v.at[t], i_send.at[j], i_recv.at[j], {"tensor": t_peer(j)})
        for j in range(1, ts)
    ]
    w_copies = []
    for c in range(cols):
        copy = pltpu.make_async_copy(w_hbm.at[:, :, c * BLK : (c + 1) * BLK], w_vmem.at[c], w_sem.at[c])
        copy.start()
        w_copies.append(copy)
    chunk_in[f] = chunk[f]

    for copy in loads[2:]:
        copy.wait()
    for r in range(row_blocks):
        gate = gate_ref[:, r * BLK : (r + 1) * BLK].astype(F32)
        up = up_ref[:, r * BLK : (r + 1) * BLK].astype(F32)
        hid[r] = (gate * jax.nn.sigmoid(gate) * up).astype(BF16)

    for copy in i_copies:
        copy.wait_recv()
    idx_copy = pltpu.make_async_copy(idx_v, idx_s, idx_sem)
    idx_copy.start()

    for copy in a_copies:
        copy.wait_recv()
    wide = [chunk_in[g].astype(F32) for g in range(fs)]
    for c in range(cols):
        panel[c] = jnp.concatenate([w[c * tok : (c + 1) * tok] for w in wide], axis=0).astype(BF16)
    idx_copy.wait()

    b_copies = []
    for q in range(groups):
        sent = []
        for j in range(1, ts):
            for k in range(per_z):
                if compact:
                    z_send[q, j, k] = panel[tile_col(t_peer(j), q * per_z + k)]
            sent.append(
                remote(
                    z_send.at[q, j] if compact else panel,
                    z_in.at[q, t],
                    b_send.at[q, j],
                    b_recv.at[q, j],
                    {"tensor": t_peer(j)},
                )
            )
        b_copies.append(sent)

    for g in range(fs):
        for k in range(CAP):
            hid_send[g, k] = hid[tile_row(k, g)]
    h_copies = over_fsdp(hid_send, hid_in, h_send, h_recv)
    hid_in[f] = hid_send[f]
    for q in range(groups):
        for k in range(per_z):
            z_in[q, t, k] = panel[tile_col(t, q * per_z + k)] if compact else panel[k]

    for copy in w_copies:
        copy.wait()
    grads = []
    p_copies = []
    for q in range(groups):
        for copy in b_copies[q]:
            copy.wait_recv()
        for m in range(per_p):
            k = q * per_p + m
            slot = m if compact else tile_col(t, k)
            wide = [z_in[q, u, slot].astype(F32) for u in range(ts)]
            pieces = [w[g * tok : (g + 1) * tok] for g in range(fs) for w in wide]
            grad = jnp.concatenate(pieces, axis=0).astype(BF16)
            grads.append(grad)
            tile = w_vmem[tile_col(t, k), tile_row(k, f)]
            out = lax.dot_general(grad, tile, (((1,), (1,)), ((), ())), preferred_element_type=F32)
            out = out.astype(BF16)
            for g in range(fs):
                prod[q, g, m] = out[g * rows : (g + 1) * rows]
        p_copies += over_fsdp(prod.at[q], prod_in.at[q], p_send.at[q], p_recv.at[q])
        prod_in[q, f] = prod[q, f]

    for copy in h_copies:
        copy.wait_recv()
    for k in range(CAP):
        left = jnp.concatenate([hid_in[g, k] for g in range(fs)], axis=0)
        total = lax.dot_general(left, grads[k], (((0,), (0,)), ((), ())), preferred_element_type=F32)
        dw[k] = (total * scale).astype(BF16)
    outs.append(pltpu.make_async_copy(dw, dw_out, out_sem.at[1]))
    outs[1].start()
    sent = [copy for group in b_copies for copy in group]
    for copy in i_copies + a_copies + sent + h_copies:
        copy.wait_send()
    for copy in p_copies:
        copy.wait_recv()
    outs.append(pltpu.make_async_copy(prod_in, pr_out, out_sem.at[2]))
    outs[2].start()
    for copy in p_copies:
        copy.wait_send()
    for copy in outs:
        copy.wait()


def finish_kernel(
    fs, idx_ref, prod_hbm, dw_hbm, gate_hbm, up_hbm, d_gate_hbm, d_up_hbm, d_weight,
    prod_ref, dw_ref, gate_ref, up_ref, acc, blank, tiled, d_gate, d_up, in_sem, z_sem, t_sem, o_sem,
):
    loads = [
        pltpu.make_async_copy(src, dst, in_sem.at[n])
        for n, (src, dst) in enumerate(
            ((dw_hbm, dw_ref), (prod_hbm, prod_ref), (gate_hbm, gate_ref), (up_hbm, up_ref))
        )
    ]
    for copy in loads:
        copy.start()
    row_blocks = acc.shape[0]
    f = lax.axis_index("fsdp")
    row_of = [idx_ref[k, f] for k in range(CAP)]
    col_of = [idx_ref[CAP + k, f] for k in range(CAP)]
    live = [idx_ref[2 * CAP + k, f] > 0 for k in range(CAP)]
    first = []
    for k in range(CAP):
        fresh = live[k]
        for m in range(k):
            fresh = fresh & jnp.logical_not(live[m] & (row_of[m] == row_of[k]))
        first.append(fresh)

    def bare(r):
        clear = None
        for k in range(CAP):
            off = jnp.logical_not(live[k] & (row_of[k] == r))
            clear = off if clear is None else clear & off
        return clear

    def fill(r):
        return pltpu.make_async_copy(blank, d_weight.at[pl.ds(r * BLK, BLK)], z_sem.at[r])

    def place(k):
        row_at = pl.multiple_of(row_of[k] * BLK, BLK)
        return pltpu.make_async_copy(tiled.at[k], d_weight.at[pl.ds(row_at, BLK)], t_sem.at[k])

    blank[...] = jnp.zeros_like(blank)
    for r in range(row_blocks):
        @pl.when(bare(r))
        def _():
            fill(r).start()

    tiled[...] = jnp.zeros_like(tiled)
    loads[0].wait()
    for k in range(CAP):
        for m in range(CAP):
            @pl.when(live[m] & (row_of[m] == row_of[k]))
            def _():
                tiled[k, :, pl.ds(pl.multiple_of(col_of[m] * BLK, BLK), BLK)] = dw_ref[m]

        @pl.when(first[k])
        def _():
            place(k).start()

    acc[...] = jnp.zeros_like(acc)
    for copy in loads[1:]:
        copy.wait()
    for g in range(fs):
        for k in range(CAP):
            row = idx_ref[k, g]
            weight = idx_ref[2 * CAP + k, g].astype(F32)
            per = prod_ref.shape[2]
            acc[row] += prod_ref[k // per, g, k % per].astype(F32) * weight
    for r in range(row_blocks):
        at = slice(r * BLK, (r + 1) * BLK)
        gate = gate_ref[:, at].astype(F32)
        up = up_ref[:, at].astype(F32)
        sig = jax.nn.sigmoid(gate)
        d_hidden = acc[r]
        d_up[:, at] = (d_hidden * gate * sig).astype(BF16)
        d_gate[:, at] = (d_hidden * up * sig * (1.0 + gate * (1.0 - sig))).astype(BF16)
    outs = [
        pltpu.make_async_copy(d_gate, d_gate_hbm, o_sem.at[0]),
        pltpu.make_async_copy(d_up, d_up_hbm, o_sem.at[1]),
    ]
    for copy in outs:
        copy.start()
    for r in range(row_blocks):
        @pl.when(bare(r))
        def _():
            fill(r).wait()

    for k in range(CAP):
        @pl.when(first[k])
        def _():
            place(k).wait()

    for copy in outs:
        copy.wait()


def per_device(out_grad, live_rows, gate_pre, up_pre, down_weight, tile_mask):
    fs = lax.axis_size("fsdp")
    ts = lax.axis_size("tensor")
    tok = out_grad.shape[0]
    rows = gate_pre.shape[0]
    row_blocks = tile_mask.shape[0]
    cols = down_weight.shape[1] // BLK
    groups = 2 if cols > CAP else 1
    per_z = CAP // groups if cols > CAP else cols
    scale = 1.0 / math.sqrt(rows * fs)
    mask = tile_mask
    if row_blocks % 8:
        mask = jnp.pad(tile_mask, ((0, 8 - row_blocks % 8), (0, 0)))
    smem = pl.BlockSpec(memory_space=pltpu.SMEM)
    hbm = pl.BlockSpec(memory_space=pltpu.HBM)
    slots = (fs, CAP, rows, BLK)
    halves = (groups, fs, CAP // groups, rows, BLK)
    blocks = (row_blocks, rows, BLK)
    dma = pltpu.SemaphoreType.DMA
    prod, tiles, lists = pl.pallas_call(
        functools.partial(exchange_kernel, fs, ts, cols, scale),
        out_shape=(
            jax.ShapeDtypeStruct(halves, BF16),
            jax.ShapeDtypeStruct((CAP, BLK, BLK), BF16),
            jax.ShapeDtypeStruct((16, BLK), jnp.int32),
        ),
        in_specs=[smem, hbm, hbm, hbm, hbm, hbm],
        out_specs=(hbm,) * 3,
        scratch_shapes=[
            pltpu.VMEM(out_grad.shape, BF16),
            pltpu.VMEM(gate_pre.shape, BF16),
            pltpu.VMEM(up_pre.shape, BF16),
            pltpu.VMEM(mask.shape, jnp.int32),
            pltpu.VMEM((CAP, BLK, BLK), BF16),
            pltpu.VMEM((fs, cols * tok, BLK), BF16),
            pltpu.VMEM((fs, cols * tok, BLK), BF16),
            pltpu.VMEM((cols, fs * tok, BLK), BF16),
            pltpu.VMEM((groups, ts, per_z, fs * tok, BLK), BF16),
            pltpu.VMEM((groups, ts, per_z, fs * tok, BLK), BF16),
            pltpu.VMEM(blocks, BF16),
            pltpu.VMEM(slots, BF16),
            pltpu.VMEM(slots, BF16),
            pltpu.VMEM(halves, BF16),
            pltpu.VMEM(halves, BF16),
            pltpu.VMEM((cols, row_blocks, BLK, BLK), BF16),
            pltpu.VMEM((ts, 16, BLK), jnp.int32),
            pltpu.SMEM((ts, 16, BLK), jnp.int32),
            dma((4,)),
            dma((3,)),
            dma((cols,)),
            dma,
            dma((ts,)),
            dma((ts,)),
            dma((fs,)),
            dma((fs,)),
            dma((groups, ts)),
            dma((groups, ts)),
            dma((fs,)),
            dma((fs,)),
            dma((groups, fs)),
            dma((groups, fs)),
        ],
        compiler_params=pltpu.CompilerParams(
            collective_id=0, has_side_effects=True, vmem_limit_bytes=60 * 1024 * 1024
        ),
        name="exchange",
    )(live_rows, out_grad, gate_pre, up_pre, mask, down_weight.reshape(row_blocks, BLK, cols * BLK))
    return pl.pallas_call(
        functools.partial(finish_kernel, fs),
        out_shape=(
            jax.ShapeDtypeStruct(gate_pre.shape, BF16),
            jax.ShapeDtypeStruct(up_pre.shape, BF16),
            jax.ShapeDtypeStruct(down_weight.shape, BF16),
        ),
        in_specs=[smem, hbm, hbm, hbm, hbm],
        out_specs=(hbm, hbm, hbm),
        scratch_shapes=[
            pltpu.VMEM(halves, BF16),
            pltpu.VMEM((CAP, BLK, BLK), BF16),
            pltpu.VMEM(gate_pre.shape, BF16),
            pltpu.VMEM(up_pre.shape, BF16),
            pltpu.VMEM(blocks, F32),
            pltpu.VMEM((BLK, down_weight.shape[1]), BF16),
            pltpu.VMEM((CAP, BLK, down_weight.shape[1]), BF16),
            pltpu.VMEM(gate_pre.shape, BF16),
            pltpu.VMEM(up_pre.shape, BF16),
            dma((4,)),
            dma((row_blocks,)),
            dma((CAP,)),
            dma((2,)),
        ],
        compiler_params=pltpu.CompilerParams(vmem_limit_bytes=60 * 1024 * 1024),
        name="finish",
    )(lists, prod, tiles, gate_pre, up_pre)


def solution(mesh):
    return jax.shard_map(
        per_device,
        mesh=mesh,
        in_specs=(
            P(("fsdp", "tensor"), None),
            P(("fsdp", "tensor")),
            P("fsdp", "tensor"),
            P("fsdp", "tensor"),
            P("tensor", "fsdp"),
            P("tensor", None),
        ),
        out_specs=(P("fsdp", "tensor"), P("fsdp", "tensor"), P("tensor", "fsdp")),
        check_vma=False,
    )
```
